128 devices in a mesh: lat: 4 (over z_hi, core), lon: 32 (over x, z_lo, y).
Axes of the slice: x: 4, y: 4, z: 4 (z_hi: 2, z_lo: 2; z = z_hi * 2 + z_lo), core: 2. Of those that a mesh axis runs over, the one named last changes fastest.
Arguments:
- queries: bfloat16 [1, 128, 512, 3072], P(None, 'lat', 'lon'), may hold values from -11 to 11
- key_value: bfloat16 [2, 1, 128, 512, 3072], P(None, None, 'lat', 'lon'), may hold values from -11 to 11
- text_kv: bfloat16 [2, 1, 512, 3072], P(None, None, ('lat', 'lon')), may hold values from -6 to 6
Outputs:
- attended: bfloat16 [1, 128, 512, 3072], P(None, 'lat', 'lon')
The draws below stay inside these ranges and needn't reach their ends.
All inputs are finite; a program needn't handle non-finite values.
Results may differ from the reference program's by a relative error of at most 0.005.
Values may be sent and summed in bfloat16 or wider, within the bound.
No kernel may reach another device: no remote copies, remote signals or barrier semaphores. Data moves between devices by JAX's collectives and lax.ppermute only.
A program may use at most 128 MiB of HBM per device.

```python
import math
import jax
import jax.numpy as jnp
from jax import lax

HEADS = 24
HD = 128
TEXT = 512
RADIUS = 8
PANOS = 1
LAT_DEV = 32
LON_DEV = 16
LAT = 128
LON = 512
CH = 3072
N_LAT = 4
N_LON = 32


def draw_queries(key, part):
    key = jax.random.fold_in(key, 3)
    shape = (PANOS, LAT, LON, CH)
    return (jnp.clip(jax.random.normal(key, shape), -4.0, 4.0) * 2.0).astype(jnp.bfloat16)


def draw_key_value(key, part):
    key = jax.random.fold_in(key, 7)
    key_part, value_part = jax.random.split(key)
    shape = (PANOS, LAT, LON, CH)
    keys = jnp.clip(jax.random.normal(key_part, shape), -4.0, 4.0)
    values = jnp.clip(jax.random.normal(value_part, shape), -4.0, 4.0)
    return jnp.stack([keys, values], axis=0).astype(jnp.bfloat16)


def levels(own_key, dims, cuts, least, largest):
    def one(axis_at, blocks):
        draws = jax.random.uniform(jax.random.fold_in(jax.random.fold_in(own_key, 6), axis_at), (blocks,), jnp.float32, least / len(cuts), largest / len(cuts))
        return jnp.repeat(jnp.exp(draws), dims[axis_at] // blocks).reshape((-1,) + (1,) * (len(dims) - axis_at - 1))

    factor_of = one(*cuts[0])
    for cut in cuts[1:]:
        factor_of = factor_of * one(*cut)
    return factor_of


def gaussian(stream_key, dims, spread, limit, shards=(), kind=jnp.bfloat16):
    loudness = levels(stream_key, dims, shards, -0.22, 0.18) if shards else 1.0
    array = jax.random.normal(stream_key, dims, jnp.float32) * spread * loudness
    return jnp.minimum(jnp.maximum(array, -limit), limit).astype(kind)


def setup_inputs(seed: int = 0) -> dict:
    key_of = jax.random.split(jax.random.key(seed), 4)
    queries = draw_queries(jax.random.fold_in(key_of[3], 71), 0)
    key_value = draw_key_value(jax.random.fold_in(key_of[3], 71), 0)
    text_kv = gaussian(key_of[2], (2, PANOS, TEXT, CH), 1.0, 6.0, ((2, 128),))
    return {"queries": queries, "key_value": key_value, "text_kv": text_kv}


def neighbor_mask(rows, cols, first_row, total_rows):
    query_row = jnp.arange(rows, dtype=jnp.int32)[:, None, None, None]
    query_col = jnp.arange(cols, dtype=jnp.int32)[None, :, None, None]
    key_row = jnp.arange(rows + 2 * RADIUS, dtype=jnp.int32)[None, None, :, None]
    key_col = jnp.arange(cols + 2 * RADIUS, dtype=jnp.int32)[None, None, None, :]
    inside = (jnp.abs(key_row - RADIUS - query_row) <= RADIUS) & (jnp.abs(key_col - RADIUS - query_col) <= RADIUS)
    global_row = first_row + key_row
    inside = inside & (global_row >= 0) & (global_row < total_rows)
    return inside.reshape(rows * cols, (rows + 2 * RADIUS) * (cols + 2 * RADIUS))

def attend_head(query_rows, near_keys, near_values, text_keys, text_values, allowed, start):
    scale = 1.0 / math.sqrt(HD)
    q_part = lax.dynamic_slice_in_dim(query_rows, start, HD, 2).astype(jnp.float32)
    nk_part = lax.dynamic_slice_in_dim(near_keys, start, HD, 2).astype(jnp.float32)
    nv_part = lax.dynamic_slice_in_dim(near_values, start, HD, 2).astype(jnp.float32)
    tk_part = lax.dynamic_slice_in_dim(text_keys, start, HD, 2).astype(jnp.float32)
    tv_part = lax.dynamic_slice_in_dim(text_values, start, HD, 2).astype(jnp.float32)
    near = jnp.einsum('pqd,pkd->pqk', q_part, nk_part) * scale
    far = jnp.einsum('pqd,pkd->pqk', q_part, tk_part) * scale
    near = jnp.where(allowed[None], near, -jnp.inf)
    top = jnp.maximum(lax.optimization_barrier(jnp.max(near, axis=-1, keepdims=True)), lax.optimization_barrier(jnp.max(far, axis=-1, keepdims=True)))
    near_exp = jnp.exp(near - top)
    far_exp = jnp.exp(far - top)
    total = lax.optimization_barrier(jnp.sum(near_exp, axis=-1, keepdims=True)) + lax.optimization_barrier(jnp.sum(far_exp, axis=-1, keepdims=True))
    near_weight = (near_exp / total).astype(jnp.bfloat16).astype(jnp.float32)
    far_weight = (far_exp / total).astype(jnp.bfloat16).astype(jnp.float32)
    result = jnp.einsum('pqk,pkd->pqd', near_weight, nv_part) + jnp.einsum('pqk,pkd->pqd', far_weight, tv_part)
    return result.astype(jnp.bfloat16)

def reference(queries, key_value, text_kv):
    span_rows = LAT_DEV + 2 * RADIUS
    span_cols = LON_DEV + 2 * RADIUS
    padded = jnp.pad(key_value, ((0, 0), (0, 0), (RADIUS, RADIUS), (0, 0), (0, 0)))
    padded = jnp.concatenate([padded[:, :, :, LON - RADIUS:], padded, padded[:, :, :, :RADIUS]], axis=3)
    text_keys = text_kv[0]
    text_values = text_kv[1]

    def one_tile(tile):
        row_block = (tile // N_LON).astype(jnp.int32)
        col_block = (tile % N_LON).astype(jnp.int32)
        row_start = (row_block * LAT_DEV).astype(jnp.int32)
        col_start = (col_block * LON_DEV).astype(jnp.int32)
        zero = jnp.zeros((), jnp.int32)
        query_tile = lax.dynamic_slice(queries, (zero, row_start, col_start, zero), (PANOS, LAT_DEV, LON_DEV, CH))
        query_rows = query_tile.reshape(PANOS, LAT_DEV * LON_DEV, CH)
        region = lax.dynamic_slice(padded, (zero, zero, row_start, col_start, zero), (2, PANOS, span_rows, span_cols, CH))
        region = region.reshape(2, PANOS, span_rows * span_cols, CH)
        allowed = neighbor_mask(LAT_DEV, LON_DEV, row_start - RADIUS, LAT)
        starts = jnp.arange(HEADS, dtype=jnp.int32) * HD
        heads_out = lax.map(lambda start: attend_head(query_rows, region[0], region[1], text_keys, text_values, allowed, start), starts)
        return jnp.transpose(heads_out, (1, 2, 0, 3)).reshape(PANOS, LAT_DEV, LON_DEV, CH)
    tiles = lax.map(one_tile, jnp.arange(N_LAT * N_LON, dtype=jnp.int32))
    tiles = tiles.reshape(N_LAT, N_LON, PANOS, LAT_DEV, LON_DEV, CH)
    tiles = jnp.transpose(tiles, (2, 0, 3, 1, 4, 5))
    return tiles.reshape(PANOS, LAT, LON, CH)
```

```python
import functools
import math

import jax
import jax.numpy as jnp
import numpy as np
from jax import lax
from jax.experimental import pallas as pl
from jax.experimental.pallas import tpu as pltpu
from jax.sharding import PartitionSpec as P

HD = 128
RADIUS = 8
NEG = -1e30
ZH, CORE, NX, ZL, NY = 2, 2, 4, 2, 4
N_LAT, N_LON = ZH * CORE, NX * ZL * NY
CHUNKS = (8, 8, 6, 2)
PER_STEP = 2
WIDE = PER_STEP * HD
BLOCK = 16


def send(x, zh=0, core=0, x_=0, zl=0, y=0):
    pairs = []
    for i in range(N_LAT * N_LON):
        c = list(np.unravel_index(i, (ZH, CORE, NX, ZL, NY)))
        t = [(a + b) % n for a, b, n in zip(c, (zh, core, x_, zl, y), (ZH, CORE, NX, ZL, NY))]
        pairs.append((i, int(np.ravel_multi_index(t, (ZH, CORE, NX, ZL, NY)))))
    return lax.ppermute(x, ("lat", "lon"), pairs)


def send_lon(x, step):
    return lax.ppermute(x, "lon", [(i, (i + step) % N_LON) for i in range(N_LON)])


def send_lat(x, step):
    return lax.ppermute(
        x, "lat", [(i, i + step) for i in range(N_LAT) if 0 <= i + step < N_LAT]
    )


def gather_prompt(text_kv):
    core = lax.axis_index("lat") % CORE
    text = text_kv[:, 0]
    mine = lax.dynamic_index_in_dim(text, core, 0, keepdims=False)
    theirs = lax.dynamic_index_in_dim(text, 1 - core, 0, keepdims=False)
    other = send(theirs, core=1)
    first = core == 0
    block = jnp.concatenate([jnp.where(first, mine, other), jnp.where(first, other, mine)], 0)[None]
    block = jnp.concatenate([block, send(block, y=1), send(block, y=3), send(block, y=2)], 0)
    block = jnp.concatenate(
        [block, send(block, zl=1), send(block, zh=1), send(block, zh=1, zl=1)], 0
    )
    up, down = send(block, x_=1), send(block, x_=3)
    half = block.shape[0] // 2
    far_a, far_b = send(up[:half], x_=1), send(down[half:], x_=3)
    own = jnp.concatenate([block, up, down, far_a, far_b], 0)
    return own, send(own, core=1)


def pack_body(own_ref, r_ref, l_ref):
    l_ref[...] = own_ref[:, 0, :, :RADIUS]
    r_ref[...] = own_ref[:, 0, :, RADIUS:]


def pack_tall_body(own_ref, top_ref, bot_ref, r_ref, l_ref):
    for ref, cols in ((l_ref, slice(0, RADIUS)), (r_ref, slice(RADIUS, 2 * RADIUS))):
        ref[:, :RADIUS] = top_ref[:, :, cols]
        ref[:, RADIUS : RADIUS + 32] = own_ref[:, 0, :, cols]
        ref[:, RADIUS + 32 :] = bot_ref[:, :, cols]


def pack(own, head, heads, edges=None):
    at = head // PER_STEP
    rows = 32 if edges is None else 48
    out = jax.ShapeDtypeStruct((2, rows, RADIUS, heads * HD), jnp.bfloat16)
    specs = [pl.BlockSpec((2, 1, 32, 16, WIDE), lambda i: (0, 0, 0, 0, at + i))]
    if edges is not None:
        specs += [pl.BlockSpec((2, RADIUS, 16, WIDE), lambda i: (0, 0, 0, at + i))] * 2
    return pl.pallas_call(
        pack_body if edges is None else pack_tall_body,
        grid=(heads // PER_STEP,),
        in_specs=specs,
        out_specs=[pl.BlockSpec((2, rows, RADIUS, WIDE), lambda i: (0, 0, 0, i))] * 2,
        out_shape=[out, out],
        compiler_params=pltpu.CompilerParams(vmem_limit_bytes=40 << 20),
    )(own, *(edges or ()))


def attend_body(tall, first_call, *refs):
    refs = list(refs)
    flip_ref, q_ref, own_ref, left_ref, right_ref, top_ref, bot_ref = refs[:7]
    del refs[:7]
    if not tall:
        tc_ref, bc_ref = refs[:2]
        del refs[:2]
    ta_ref, tb_ref, e_ref, f_ref = refs[:4]
    del refs[:4]
    if not first_call:
        del refs[:1]
    o_ref, keys_s, vals_s, tvals_s = refs
    rows, cols = 32, 16

    @pl.when(pl.program_id(0) == 0)
    def _():
        keys_s[:, :, HD:] = f_ref[...]
        vals_s[:, :, HD:] = jnp.ones((48, 32, HD), jnp.bfloat16)
        tvals_s[:, HD:] = jnp.ones((512, HD), jnp.bfloat16)

    scale = math.log2(math.e) / math.sqrt(HD)
    nt = (((1,), (1,)), ((), ()))
    flip = flip_ref[0] == 1
    for head in range(PER_STEP):
        hs = slice(head * HD, (head + 1) * HD)
        for kv, dst in ((0, keys_s), (1, vals_s)):
            left, right = left_ref[kv, :, :, hs], right_ref[kv, :, :, hs]
            top, bot, own = top_ref[kv, :, :, hs], bot_ref[kv, :, :, hs], own_ref[kv, 0, :, :, hs]
            if tall:
                middle = jnp.concatenate([top, own, bot], axis=0)
                dst[:, :, :HD] = jnp.concatenate([left, middle, right], axis=1)
            else:
                dst[8:40, :, :HD] = jnp.concatenate([left, own, right], axis=1)
                dst[0:8, :, :HD] = jnp.concatenate(
                    [tc_ref[0, kv, :, :, hs], top, tc_ref[1, kv, :, :, hs]], axis=1
                )
                dst[40:48, :, :HD] = jnp.concatenate(
                    [bc_ref[0, kv, :, :, hs], bot, bc_ref[1, kv, :, :, hs]], axis=1
                )
        a, b = ta_ref[:, :, hs].reshape(512, HD), tb_ref[:, :, hs].reshape(512, HD)
        text_keys = jnp.where(flip, b, a)
        tvals_s[:, :HD] = jnp.where(flip, a, b)
        for r in range(rows // BLOCK):
            q = q_ref[0, r * BLOCK : (r + 1) * BLOCK, :, hs].reshape(BLOCK * cols, HD)
            q_wide = jnp.concatenate([q, e_ref[r * BLOCK * cols : (r + 1) * BLOCK * cols]], axis=1)
            span = BLOCK + 2 * RADIUS
            keys = keys_s[r * BLOCK : r * BLOCK + span].reshape(span * 32, 2 * HD)
            vals = vals_s[r * BLOCK : r * BLOCK + span].reshape(span * 32, 2 * HD)
            near = lax.dot_general(q_wide, keys, nt, preferred_element_type=jnp.float32)
            far = lax.dot_general(q, text_keys, nt, preferred_element_type=jnp.float32)
            top = jnp.maximum(
                jnp.max(near, -1, keepdims=True), jnp.max(far, -1, keepdims=True)
            )
            near = jnp.exp2((near - top) * scale).astype(jnp.bfloat16)
            far = jnp.exp2((far - top) * scale).astype(jnp.bfloat16)
            out = jnp.dot(near, vals, preferred_element_type=jnp.float32)
            out = out + jnp.dot(far, tvals_s[...], preferred_element_type=jnp.float32)
            out = (out[:, :HD] / out[:, HD:]).astype(jnp.bfloat16)
            o_ref[0, r * BLOCK : (r + 1) * BLOCK, :, hs] = out.reshape(BLOCK, cols, HD)


def attend(flip, queries, own, left, right, top, bot, corners, text, feats, output, head, heads):
    at = head // PER_STEP
    tall = corners is None
    rows = 48 if tall else 32
    spec = pl.BlockSpec
    in_specs = [
        spec(memory_space=pltpu.SMEM),
        spec((1, 32, 16, WIDE), lambda i: (0, 0, 0, at + i)),
        spec((2, 1, 32, 16, WIDE), lambda i: (0, 0, 0, 0, at + i)),
        spec((2, rows, RADIUS, WIDE), lambda i: (0, 0, 0, i)),
        spec((2, rows, RADIUS, WIDE), lambda i: (0, 0, 0, i)),
        spec((2, RADIUS, 16, WIDE), lambda i: (0, 0, 0, at + i)),
        spec((2, RADIUS, 16, WIDE), lambda i: (0, 0, 0, at + i)),
    ]
    args = [flip, queries, own, left, right, top, bot]
    if not tall:
        in_specs += [spec((2, 2, RADIUS, RADIUS, WIDE), lambda i: (0, 0, 0, 0, i))] * 2
        args += corners
    in_specs += [
        spec((64, 8, WIDE), lambda i: (0, 0, at + i)),
        spec((64, 8, WIDE), lambda i: (0, 0, at + i)),
        spec((512, HD), lambda i: (0, 0)),
        spec((48, 32, HD), lambda i: (0, 0, 0)),
    ]
    args += [*text, *feats]
    aliases = {}
    if output is not None:
        aliases = {len(args): 0}
        in_specs.append(spec(memory_space=pl.ANY))
        args.append(output)
    return pl.pallas_call(
        functools.partial(attend_body, tall, output is None),
        grid=(heads // PER_STEP,),
        in_specs=in_specs,
        out_specs=spec((1, 32, 16, WIDE), lambda i: (0, 0, 0, at + i)),
        out_shape=jax.ShapeDtypeStruct(queries.shape, jnp.bfloat16),
        scratch_shapes=[
            pltpu.VMEM((48, 32, 2 * HD), jnp.bfloat16),
            pltpu.VMEM((48, 32, 2 * HD), jnp.bfloat16),
            pltpu.VMEM((512, 2 * HD), jnp.bfloat16),
        ],
        input_output_aliases=aliases,
        compiler_params=pltpu.CompilerParams(vmem_limit_bytes=40 << 20),
        cost_estimate=pl.CostEstimate(
            flops=heads * 1_500_000_000, bytes_accessed=heads << 20, transcendentals=0
        ),
    )(*args)


def features():
    query = np.arange(512)
    lane = np.arange(HD)
    hot = (
        (lane[None] == (query % 16)[:, None])
        | (lane[None] - 16 == (query // 16)[:, None])
        | (lane[None] == 48)
    )
    row = jnp.arange(48, dtype=jnp.int32)[:, None, None] - RADIUS
    col = jnp.arange(32, dtype=jnp.int32)[None, :, None] - RADIUS
    lane = jnp.arange(HD, dtype=jnp.int32)[None, None, :]
    grid_row = lax.axis_index("lat") * 32 + row
    bad = (lane < 16) & (jnp.abs(col - lane) > RADIUS)
    bad |= (lane >= 16) & (lane < 48) & (jnp.abs(row - (lane - 16)) > RADIUS)
    bad |= (lane == 48) & ((grid_row < 0) | (grid_row >= N_LAT * 32))
    return jnp.asarray(hot, jnp.bfloat16), jnp.where(bad, NEG, 0.0).astype(jnp.bfloat16)


def on_device(queries, key_value, text_kv):
    flip = (lax.axis_index("lat") % CORE).astype(jnp.int32)[None]
    starts = [sum(CHUNKS[:i]) for i in range(len(CHUNKS))]
    feats = features()
    top = send_lat(key_value[:, 0, -RADIUS:], 1)
    bot = send_lat(key_value[:, 0, :RADIUS], -1)
    sides = []
    for head, heads in zip(starts, CHUNKS):
        last = head == starts[-1]
        r, l = pack(key_value, head, heads, (top, bot) if last else None)
        sides.append((send_lon(r, 1), send_lon(l, -1)))
    text = gather_prompt(text_kv)
    output = None
    for head, heads, (left, right) in zip(starts, CHUNKS, sides):
        corners = None
        if head != starts[-1]:
            down = jnp.stack([left[:, -RADIUS:], right[:, -RADIUS:]])
            up = jnp.stack([left[:, :RADIUS], right[:, :RADIUS]])
            corners = [send_lat(down, 1), send_lat(up, -1)]
        output = attend(
            flip, queries, key_value, left, right, top, bot, corners, text, feats, output, head, heads
        )
    return output


def solution(mesh):
    in_specs = (
        P(None, "lat", "lon", None),
        P(None, None, "lat", "lon", None),
        P(None, None, ("lat", "lon"), None),
    )
    out_specs = P(None, "lat", "lon", None)
    return jax.shard_map(
        on_device, mesh=mesh, in_specs=in_specs, out_specs=out_specs, check_vma=False
    )
```

```python
import functools
import math

import jax
import jax.numpy as jnp
import numpy as np
from jax import lax
from jax.experimental import pallas as pl
from jax.experimental.pallas import tpu as pltpu
from jax.sharding import PartitionSpec as P

HD = 128
RADIUS = 8
NEG = -1e30
ZH, CORE, NX, ZL, NY = 2, 2, 4, 2, 4
N_LAT, N_LON = ZH * CORE, NX * ZL * NY
CHUNKS = (4, 8, 8, 4)
PER_STEP = 4
WIDE = PER_STEP * HD
BLOCK = 16
VMEM_LIMIT = 60 << 20
PIECES = 8


def send_where(x, use, zh=0, core=0, lon=0):
    pairs = []
    for i in range(N_LAT * N_LON):
        lat, at = divmod(i, N_LON)
        a, b = divmod(lat, CORE)
        if use(a, b):
            lat = (a + zh) % ZH * CORE + (b + core) % CORE
            pairs.append((i, lat * N_LON + (at + lon) % N_LON))
    return lax.ppermute(x, ("lat", "lon"), pairs)


def send(x, zh=0, core=0, x_=0, zl=0, y=0):
    pairs = []
    for i in range(N_LAT * N_LON):
        c = list(np.unravel_index(i, (ZH, CORE, NX, ZL, NY)))
        t = [(a + b) % n for a, b, n in zip(c, (zh, core, x_, zl, y), (ZH, CORE, NX, ZL, NY))]
        pairs.append((i, int(np.ravel_multi_index(t, (ZH, CORE, NX, ZL, NY)))))
    return lax.ppermute(x, ("lat", "lon"), pairs)


def send_lon(x, step):
    return lax.ppermute(x, "lon", [(i, (i + step) % N_LON) for i in range(N_LON)])


def glue(body, out_shapes, args, deps, specs=None, out_specs=None, grid=None):
    if specs is None:
        specs = [pl.BlockSpec(memory_space=pltpu.VMEM)] * len(args)
        out_specs = [pl.BlockSpec(memory_space=pltpu.VMEM)] * len(out_shapes)
    count = len(args)

    def kernel(*refs):
        body(*refs[:count], *refs[count + len(deps) :])

    return pl.pallas_call(
        kernel,
        grid=grid or (),
        in_specs=list(specs) + [pl.BlockSpec(memory_space=pl.ANY)] * len(deps),
        out_specs=out_specs,
        out_shape=[jax.ShapeDtypeStruct(shape, jnp.bfloat16) for shape in out_shapes],
        compiler_params=pltpu.CompilerParams(vmem_limit_bytes=VMEM_LIMIT),
        cost_estimate=pl.CostEstimate(flops=1000, bytes_accessed=1000, transcendentals=0),
    )(*args, *deps)


def pack_sides(own, head, heads, deps):
    wide = 4 * HD
    at = head * HD // wide

    def body(own_ref, r_ref, l_ref):
        r_ref[...] = own_ref[:, 0, :, RADIUS:]
        l_ref[...] = own_ref[:, 0, :, :RADIUS]

    specs = [pl.BlockSpec((2, 1, 32, 16, wide), lambda i: (0, 0, 0, 0, at + i))]
    out_specs = [pl.BlockSpec((2, 32, RADIUS, wide), lambda i: (0, 0, 0, i))] * 2
    shape = (2, 32, RADIUS, heads * HD)
    return glue(body, [shape] * 2, [own], deps, specs, out_specs, (heads * HD // wide,))


def carry(arrays, deps):
    def body(*refs):
        for src, dst in zip(refs[: len(arrays)], refs[len(arrays) :]):
            dst[...] = src[...]

    return glue(body, [x.shape for x in arrays], list(arrays), deps)


def pack_far_sides(far, deps):
    def body(far_ref, r_ref, l_ref):
        r_ref[...] = far_ref[:, :, RADIUS:]
        l_ref[...] = far_ref[:, :, :RADIUS]

    specs = [pl.BlockSpec((2, RADIUS, 16, 3072), lambda i: (0, 0, 0, i))]
    out_specs = [pl.BlockSpec((2, RADIUS, RADIUS, 3072), lambda i: (0, 0, 0, i))] * 2
    return glue(body, [(2, RADIUS, RADIUS, 3072)] * 2, [far], deps, specs, out_specs, (1,))


def pack_rows(flip, own, deps):
    def body(flip_ref, first_ref, last_ref, near_ref, far_ref):
        odd = flip_ref[0] == 1
        near_ref[...] = jnp.where(odd, first_ref[:, 0], last_ref[:, 0])
        far_ref[...] = jnp.where(odd, last_ref[:, 0], first_ref[:, 0])

    specs = [
        pl.BlockSpec(memory_space=pltpu.SMEM),
        pl.BlockSpec((2, 1, RADIUS, 16, 1024), lambda i: (0, 0, 0, 0, i)),
        pl.BlockSpec((2, 1, RADIUS, 16, 1024), lambda i: (0, 0, 3, 0, i)),
    ]
    out_specs = [pl.BlockSpec((2, RADIUS, 16, 1024), lambda i: (0, 0, 0, i))] * 2
    return glue(body, [(2, RADIUS, 16, 3072)] * 2, [flip, own, own], deps, specs, out_specs, (3,))


def pack_corners(flip, left, right, deps):
    width = left.shape[-1]

    def body(flip_ref, lt_ref, lb_ref, rt_ref, rb_ref, out_ref):
        odd = flip_ref[0] == 1
        out_ref[0] = jnp.where(odd, lt_ref[...], lb_ref[...])
        out_ref[1] = jnp.where(odd, rt_ref[...], rb_ref[...])

    at_first = pl.BlockSpec((2, RADIUS, RADIUS, width), lambda i: (0, 0, 0, i))
    at_last = pl.BlockSpec((2, RADIUS, RADIUS, width), lambda i: (0, 3, 0, i))
    return glue(
        body,
        [(2, 2, RADIUS, RADIUS, width)],
        [flip, left, left, right, right],
        deps,
        [pl.BlockSpec(memory_space=pltpu.SMEM), at_first, at_last, at_first, at_last],
        [pl.BlockSpec((2, 2, RADIUS, RADIUS, width), lambda i: (0, 0, 0, 0, i))],
        (1,),
    )[0]


def prompt_stack(text, others, deps):
    def body(*refs):
        for i, ref in enumerate(refs[:-1]):
            refs[-1][i] = ref[:, 0]

    return glue(body, [(4, 2, 4, 3072)], [text, *others], deps)[0]


def prompt_split(flip, block, others, deps):
    def body(flip_ref, *refs):
        mine_ref, theirs_ref = refs[-2:]
        odd = flip_ref[0] == 1
        for half in (0, 1):
            a_ref, b_ref = refs[2 * half : 2 * half + 2]
            for i in range(4):
                keys = jnp.concatenate([a_ref[i, 0], b_ref[i, 0]], axis=0)
                values = jnp.concatenate([a_ref[i, 1], b_ref[i, 1]], axis=0)
                mine_ref[4 * half + i] = jnp.where(odd, values, keys)
                theirs_ref[4 * half + i] = jnp.where(odd, keys, values)

    whole = pl.BlockSpec(memory_space=pltpu.VMEM)
    return glue(
        body,
        [(8, 8, 3072)] * 2,
        [flip, block, *others],
        deps,
        [pl.BlockSpec(memory_space=pltpu.SMEM)] + [whole] * 4,
        [whole] * 2,
    )


def attend_body(unused, *refs):
    refs = list(refs)
    flip_ref, q_ref, own_ref, left_ref, right_ref, near_ref, far_ref = refs[:7]
    corner_ref, far_left_ref, far_right_ref = refs[7:10]
    del refs[:10]
    ta_refs, tb_refs = refs[:PIECES], refs[PIECES : 2 * PIECES]
    del refs[: 2 * PIECES]
    e_ref, f_ref = refs[:2]
    del refs[:2]
    del refs[:unused]
    o_ref, keys_s, vals_s, tvals_s = refs
    rows, cols = 32, 16

    @pl.when(pl.program_id(0) == 0)
    def _():
        keys_s[:, :, HD:] = f_ref[...]
        vals_s[:, :, HD:] = jnp.ones((48, 32, HD), jnp.bfloat16)
        tvals_s[:, HD:] = jnp.ones((512, HD), jnp.bfloat16)

    scale = math.log2(math.e) / math.sqrt(HD)
    nt = (((1,), (1,)), ((), ()))
    flip = flip_ref[0] == 1
    for head in range(PER_STEP):
        hs = slice(head * HD, (head + 1) * HD)
        for kv, dst in ((0, keys_s), (1, vals_s)):
            left, right = left_ref[kv, :, :, hs], right_ref[kv, :, :, hs]
            own = own_ref[kv, 0, :, :, hs]
            dst[8:40, :, :HD] = jnp.concatenate([left, own, right], axis=1)
            near = [corner_ref[0, kv, :, :, hs], near_ref[kv, :, :, hs], corner_ref[1, kv, :, :, hs]]
            far = [far_left_ref[kv, :, :, hs], far_ref[kv, :, :, hs], far_right_ref[kv, :, :, hs]]
            near, far = jnp.concatenate(near, axis=1), jnp.concatenate(far, axis=1)
            dst[0:8, :, :HD] = jnp.where(flip, near, far)
            dst[40:48, :, :HD] = jnp.where(flip, far, near)
        a = jnp.concatenate([ref[:, :, hs].reshape(64, HD) for ref in ta_refs], axis=0)
        b = jnp.concatenate([ref[:, :, hs].reshape(64, HD) for ref in tb_refs], axis=0)
        text_keys = jnp.where(flip, b, a)
        tvals_s[:, :HD] = jnp.where(flip, a, b)
        for r in range(rows // BLOCK):
            q = q_ref[0, r * BLOCK : (r + 1) * BLOCK, :, hs].reshape(BLOCK * cols, HD)
            q_wide = jnp.concatenate([q, e_ref[r * BLOCK * cols : (r + 1) * BLOCK * cols]], axis=1)
            span = BLOCK + 2 * RADIUS
            keys = keys_s[r * BLOCK : r * BLOCK + span].reshape(span * 32, 2 * HD)
            vals = vals_s[r * BLOCK : r * BLOCK + span].reshape(span * 32, 2 * HD)
            near = lax.dot_general(q_wide, keys, nt, preferred_element_type=jnp.float32)
            far = lax.dot_general(q, text_keys, nt, preferred_element_type=jnp.float32)
            top = jnp.maximum(
                jnp.max(near, -1, keepdims=True), jnp.max(far, -1, keepdims=True)
            )
            near = jnp.exp2((near - top) * scale).astype(jnp.bfloat16)
            far = jnp.exp2((far - top) * scale).astype(jnp.bfloat16)
            out = jnp.dot(near, vals, preferred_element_type=jnp.float32)
            out = out + jnp.dot(far, tvals_s[...], preferred_element_type=jnp.float32)
            out = (out[:, :HD] / out[:, HD:]).astype(jnp.bfloat16)
            o_ref[0, r * BLOCK : (r + 1) * BLOCK, :, hs] = out.reshape(BLOCK, cols, HD)


def attend(flip, queries, own, sides, rows, corner, far_sides, text, feats, output, head, heads, deps):
    at = head // PER_STEP
    spec = pl.BlockSpec
    in_specs = [
        spec(memory_space=pltpu.SMEM),
        spec((1, 32, 16, WIDE), lambda i: (0, 0, 0, at + i)),
        spec((2, 1, 32, 16, WIDE), lambda i: (0, 0, 0, 0, at + i)),
        spec((2, 32, RADIUS, WIDE), lambda i: (0, 0, 0, i)),
        spec((2, 32, RADIUS, WIDE), lambda i: (0, 0, 0, i)),
        spec((2, RADIUS, 16, WIDE), lambda i: (0, 0, 0, at + i)),
        spec((2, RADIUS, 16, WIDE), lambda i: (0, 0, 0, at + i)),
        spec((2, 2, RADIUS, RADIUS, WIDE), lambda i: (0, 0, 0, 0, i)),
        spec((2, RADIUS, RADIUS, WIDE), lambda i: (0, 0, 0, at + i)),
        spec((2, RADIUS, RADIUS, WIDE), lambda i: (0, 0, 0, at + i)),
    ]
    args = [flip, queries, own, *sides, *rows, corner, *far_sides]
    in_specs += [spec((8, 8, WIDE), lambda i: (0, 0, at + i))] * (2 * PIECES)
    in_specs += [
        spec((512, HD), lambda i: (0, 0)),
        spec((48, 32, HD), lambda i: (0, 0, 0)),
    ]
    args += [*text, *feats]
    aliases = {}
    if output is not None:
        aliases = {len(args): 0}
        in_specs.append(spec(memory_space=pl.ANY))
        args.append(output)
    in_specs += [spec(memory_space=pl.ANY)] * len(deps)
    args += deps
    return pl.pallas_call(
        functools.partial(attend_body, len(deps) + (output is not None)),
        grid=(heads // PER_STEP,),
        in_specs=in_specs,
        out_specs=spec((1, 32, 16, WIDE), lambda i: (0, 0, 0, at + i)),
        out_shape=jax.ShapeDtypeStruct(queries.shape, jnp.bfloat16),
        scratch_shapes=[
            pltpu.VMEM((48, 32, 2 * HD), jnp.bfloat16),
            pltpu.VMEM((48, 32, 2 * HD), jnp.bfloat16),
            pltpu.VMEM((512, 2 * HD), jnp.bfloat16),
        ],
        input_output_aliases=aliases,
        compiler_params=pltpu.CompilerParams(vmem_limit_bytes=VMEM_LIMIT),
        cost_estimate=pl.CostEstimate(
            flops=1000, bytes_accessed=1000, transcendentals=0
        ),
    )(*args)


def features():
    query = np.arange(512)
    lane = np.arange(HD)
    hot = (
        (lane[None] == (query % 16)[:, None])
        | (lane[None] - 16 == (query // 16)[:, None])
        | (lane[None] == 48)
    )
    row = jnp.arange(48, dtype=jnp.int32)[:, None, None] - RADIUS
    col = jnp.arange(32, dtype=jnp.int32)[None, :, None] - RADIUS
    lane = jnp.arange(HD, dtype=jnp.int32)[None, None, :]
    grid_row = lax.axis_index("lat") * 32 + row
    bad = (lane < 16) & (jnp.abs(col - lane) > RADIUS)
    bad |= (lane >= 16) & (lane < 48) & (jnp.abs(row - (lane - 16)) > RADIUS)
    bad |= (lane == 48) & ((grid_row < 0) | (grid_row >= N_LAT * 32))
    return jnp.asarray(hot, jnp.bfloat16), jnp.where(bad, NEG, 0.0).astype(jnp.bfloat16)


def on_device(queries, key_value, text_kv):
    flip = (lax.axis_index("lat") % CORE).astype(jnp.int32)[None]
    starts = [sum(CHUNKS[:i]) for i in range(len(CHUNKS))]
    feats = features()
    corners = [None] * len(CHUNKS)

    def inner(a, b):
        return a != b

    def send_corners(i, deps):
        rows = pack_corners(flip, *sides[i], deps)
        corners[i] = send(rows, core=1)
        return rows

    sides = []

    def send_sides(i, deps):
        r, l = pack_sides(key_value, starts[i], CHUNKS[i], deps)
        sides.append((send_lon(r, 1), send_lon(l, -1)))
        return r

    by_z = [send(text_kv, zl=1), send(text_kv, zh=1), send(text_kv, zh=1, zl=1)]
    block = prompt_stack(text_kv, by_z, ())
    by_y = [send(block, y=step) for step in (1, 3, 2)]
    near, far = pack_rows(flip, key_value, (block,))
    mine, theirs = prompt_split(flip, block, by_y, (near,))
    other = send(theirs, core=1)
    near, far = send(near, core=1), send_where(far, inner, zh=1, core=1)
    up, down = [send(x, x_=1) for x in (mine, other)], [send(x, x_=3) for x in (mine, other)]
    pieces = [mine, other, *up, *down, send(up[0], x_=1), send(down[1], x_=3)]
    swapped = [send(piece, core=1) for piece in pieces]
    text = pieces + [swapped[i ^ 1] for i in range(PIECES)]
    token = send_sides(0, (up[0], down[1]))
    token = send_sides(1, (token,))
    r, l = pack_far_sides(far, (token,))
    far_sides = (send_where(r, inner, lon=1), send_where(l, inner, lon=-1))
    token = send_sides(2, (r,))
    token = send_sides(3, (token,))
    output = None
    for i in range(len(CHUNKS)):
        token = send_corners(i, (token,))
        output = token = attend(
            flip, queries, key_value, sides[i], (near, far), corners[i], far_sides, text, feats,
            output, starts[i], CHUNKS[i], (),
        )
    return output


def solution(mesh):
    in_specs = (
        P(None, "lat", "lon", None),
        P(None, None, "lat", "lon", None),
        P(None, None, ("lat", "lon"), None),
    )
    out_specs = P(None, "lat", "lon", None)
    return jax.shard_map(
        on_device, mesh=mesh, in_specs=in_specs, out_specs=out_specs, check_vma=False
    )
```

```python
import functools
import math

import jax
import jax.numpy as jnp
import numpy as np
from jax import lax
from jax.experimental import pallas as pl
from jax.experimental.pallas import tpu as pltpu
from jax.sharding import PartitionSpec as P

HD = 128
RADIUS = 8
NEG = -1e30
ZH, CORE, NX, ZL, NY = 2, 2, 4, 2, 4
N_LAT, N_LON = ZH * CORE, NX * ZL * NY
CHUNKS = (4, 8, 8, 4)
PER_STEP = 4
WIDE = PER_STEP * HD
BLOCK = 16
VMEM_LIMIT = 66_800_000
PIECES = 8


def send_where(x, use, zh=0, core=0, lon=0):
    pairs = []
    for i in range(N_LAT * N_LON):
        lat, at = divmod(i, N_LON)
        a, b = divmod(lat, CORE)
        if use(a, b):
            lat = (a + zh) % ZH * CORE + (b + core) % CORE
            pairs.append((i, lat * N_LON + (at + lon) % N_LON))
    return lax.ppermute(x, ("lat", "lon"), pairs)


def send(x, zh=0, core=0, x_=0, zl=0, y=0):
    pairs = []
    for i in range(N_LAT * N_LON):
        c = list(np.unravel_index(i, (ZH, CORE, NX, ZL, NY)))
        t = [(a + b) % n for a, b, n in zip(c, (zh, core, x_, zl, y), (ZH, CORE, NX, ZL, NY))]
        pairs.append((i, int(np.ravel_multi_index(t, (ZH, CORE, NX, ZL, NY)))))
    return lax.ppermute(x, ("lat", "lon"), pairs)


def send_lon(x, step):
    return lax.ppermute(x, "lon", [(i, (i + step) % N_LON) for i in range(N_LON)])


def glue(body, out_shapes, args, deps, specs=None, out_specs=None, grid=None):
    if specs is None:
        specs = [pl.BlockSpec(memory_space=pltpu.VMEM)] * len(args)
        out_specs = [pl.BlockSpec(memory_space=pltpu.VMEM)] * len(out_shapes)
    count = len(args)

    def kernel(*refs):
        body(*refs[:count], *refs[count + len(deps) :])

    return pl.pallas_call(
        kernel,
        grid=grid or (),
        in_specs=list(specs) + [pl.BlockSpec(memory_space=pl.ANY)] * len(deps),
        out_specs=out_specs,
        out_shape=[jax.ShapeDtypeStruct(shape, jnp.bfloat16) for shape in out_shapes],
        compiler_params=pltpu.CompilerParams(vmem_limit_bytes=VMEM_LIMIT),
        cost_estimate=pl.CostEstimate(flops=1000, bytes_accessed=1000, transcendentals=0),
    )(*args, *deps)


def pack_sides(own, head, heads, deps):
    wide = 4 * HD
    at = head * HD // wide

    def body(own_ref, r_ref, l_ref):
        r_ref[...] = own_ref[:, 0, :, RADIUS:]
        l_ref[...] = own_ref[:, 0, :, :RADIUS]

    specs = [pl.BlockSpec((2, 1, 32, 16, wide), lambda i: (0, 0, 0, 0, at + i))]
    out_specs = [pl.BlockSpec((2, 32, RADIUS, wide), lambda i: (0, 0, 0, i))] * 2
    shape = (2, 32, RADIUS, heads * HD)
    return glue(body, [shape] * 2, [own], deps, specs, out_specs, (heads * HD // wide,))


def carry(arrays, deps):
    def body(*refs):
        for src, dst in zip(refs[: len(arrays)], refs[len(arrays) :]):
            dst[...] = src[...]

    return glue(body, [x.shape for x in arrays], list(arrays), deps)


def pack_far_sides(far, deps):
    def body(far_ref, r_ref, l_ref):
        r_ref[...] = far_ref[:, :, RADIUS:]
        l_ref[...] = far_ref[:, :, :RADIUS]

    specs = [pl.BlockSpec((2, RADIUS, 16, 3072), lambda i: (0, 0, 0, i))]
    out_specs = [pl.BlockSpec((2, RADIUS, RADIUS, 3072), lambda i: (0, 0, 0, i))] * 2
    return glue(body, [(2, RADIUS, RADIUS, 3072)] * 2, [far], deps, specs, out_specs, (1,))


def pack_rows(flip, own, deps):
    def body(flip_ref, first_ref, last_ref, near_ref, far_ref):
        odd = flip_ref[0] == 1
        near_ref[...] = jnp.where(odd, first_ref[:, 0], last_ref[:, 0])
        far_ref[...] = jnp.where(odd, last_ref[:, 0], first_ref[:, 0])

    specs = [
        pl.BlockSpec(memory_space=pltpu.SMEM),
        pl.BlockSpec((2, 1, RADIUS, 16, 1024), lambda i: (0, 0, 0, 0, i)),
        pl.BlockSpec((2, 1, RADIUS, 16, 1024), lambda i: (0, 0, 3, 0, i)),
    ]
    out_specs = [pl.BlockSpec((2, RADIUS, 16, 1024), lambda i: (0, 0, 0, i))] * 2
    return glue(body, [(2, RADIUS, 16, 3072)] * 2, [flip, own, own], deps, specs, out_specs, (3,))


def pack_corners(flip, left, right, deps):
    width = left.shape[-1]

    def body(flip_ref, lt_ref, lb_ref, rt_ref, rb_ref, out_ref):
        odd = flip_ref[0] == 1
        out_ref[0] = jnp.where(odd, lt_ref[...], lb_ref[...])
        out_ref[1] = jnp.where(odd, rt_ref[...], rb_ref[...])

    at_first = pl.BlockSpec((2, RADIUS, RADIUS, width), lambda i: (0, 0, 0, i))
    at_last = pl.BlockSpec((2, RADIUS, RADIUS, width), lambda i: (0, 3, 0, i))
    return glue(
        body,
        [(2, 2, RADIUS, RADIUS, width)],
        [flip, left, left, right, right],
        deps,
        [pl.BlockSpec(memory_space=pltpu.SMEM), at_first, at_last, at_first, at_last],
        [pl.BlockSpec((2, 2, RADIUS, RADIUS, width), lambda i: (0, 0, 0, 0, i))],
        (1,),
    )[0]


def prompt_stack(text, others, deps):
    def body(*refs):
        for i, ref in enumerate(refs[:-1]):
            refs[-1][i] = ref[:, 0]

    return glue(body, [(4, 2, 4, 3072)], [text, *others], deps)[0]


def prompt_split(flip, block, others, deps):
    def body(flip_ref, *refs):
        mine_ref, theirs_ref = refs[-2:]
        odd = flip_ref[0] == 1
        for half in (0, 1):
            a_ref, b_ref = refs[2 * half : 2 * half + 2]
            for i in range(4):
                keys = jnp.concatenate([a_ref[i, 0], b_ref[i, 0]], axis=0)
                values = jnp.concatenate([a_ref[i, 1], b_ref[i, 1]], axis=0)
                mine_ref[4 * half + i] = jnp.where(odd, values, keys)
                theirs_ref[4 * half + i] = jnp.where(odd, keys, values)

    whole = pl.BlockSpec(memory_space=pltpu.VMEM)
    return glue(
        body,
        [(8, 8, 3072)] * 2,
        [flip, block, *others],
        deps,
        [pl.BlockSpec(memory_space=pltpu.SMEM)] + [whole] * 4,
        [whole] * 2,
    )


def attend_body(unused, *refs):
    refs = list(refs)
    flip_ref, q_ref, own_ref, left_ref, right_ref, near_ref, far_ref = refs[:7]
    corner_ref, far_left_ref, far_right_ref = refs[7:10]
    del refs[:10]
    ta_refs, tb_refs = refs[:PIECES], refs[PIECES : 2 * PIECES]
    del refs[: 2 * PIECES]
    e_ref, f_ref = refs[:2]
    del refs[:2]
    del refs[:unused]
    o_ref, keys_s, vals_s, tvals_s = refs
    rows, cols = 32, 16

    @pl.when(pl.program_id(0) == 0)
    def _():
        keys_s[:, :, HD:] = f_ref[...]
        vals_s[:, :, HD:] = jnp.ones((48, 32, HD), jnp.bfloat16)
        tvals_s[:, HD:] = jnp.ones((512, HD), jnp.bfloat16)

    scale = math.log2(math.e) / math.sqrt(HD)
    nt = (((1,), (1,)), ((), ()))
    flip = flip_ref[0] == 1
    for head in range(PER_STEP):
        hs = slice(head * HD, (head + 1) * HD)
        for kv, dst in ((0, keys_s), (1, vals_s)):
            left, right = left_ref[kv, :, :, hs], right_ref[kv, :, :, hs]
            own = own_ref[kv, 0, :, :, hs]
            dst[8:40, :, :HD] = jnp.concatenate([left, own, right], axis=1)
            near = [corner_ref[0, kv, :, :, hs], near_ref[kv, :, :, hs], corner_ref[1, kv, :, :, hs]]
            far = [far_left_ref[kv, :, :, hs], far_ref[kv, :, :, hs], far_right_ref[kv, :, :, hs]]
            near, far = jnp.concatenate(near, axis=1), jnp.concatenate(far, axis=1)
            dst[0:8, :, :HD] = jnp.where(flip, near, far)
            dst[40:48, :, :HD] = jnp.where(flip, far, near)
        a = jnp.concatenate([ref[:, :, hs].reshape(64, HD) for ref in ta_refs], axis=0)
        b = jnp.concatenate([ref[:, :, hs].reshape(64, HD) for ref in tb_refs], axis=0)
        text_keys = jnp.where(flip, b, a)
        tvals_s[:, :HD] = jnp.where(flip, a, b)
        for r in range(rows // BLOCK):
            q = q_ref[0, r * BLOCK : (r + 1) * BLOCK, :, hs].reshape(BLOCK * cols, HD)
            q_wide = jnp.concatenate([q, e_ref[r * BLOCK * cols : (r + 1) * BLOCK * cols]], axis=1)
            span = BLOCK + 2 * RADIUS
            keys = keys_s[r * BLOCK : r * BLOCK + span].reshape(span * 32, 2 * HD)
            vals = vals_s[r * BLOCK : r * BLOCK + span].reshape(span * 32, 2 * HD)
            near = lax.dot_general(q_wide, keys, nt, preferred_element_type=jnp.float32)
            far = lax.dot_general(q, text_keys, nt, preferred_element_type=jnp.float32)
            top = jnp.maximum(
                jnp.max(near, -1, keepdims=True), jnp.max(far, -1, keepdims=True)
            )
            near = jnp.exp2((near - top) * scale).astype(jnp.bfloat16)
            far = jnp.exp2((far - top) * scale).astype(jnp.bfloat16)
            out = jnp.dot(near, vals, preferred_element_type=jnp.float32)
            out = out + jnp.dot(far, tvals_s[...], preferred_element_type=jnp.float32)
            out = (out[:, :HD] / out[:, HD:]).astype(jnp.bfloat16)
            o_ref[0, r * BLOCK : (r + 1) * BLOCK, :, hs] = out.reshape(BLOCK, cols, HD)


def attend(flip, queries, own, sides, rows, corner, far_sides, text, feats, output, head, heads, deps):
    at = head // PER_STEP
    spec = pl.BlockSpec
    in_specs = [
        spec(memory_space=pltpu.SMEM),
        spec((1, 32, 16, WIDE), lambda i: (0, 0, 0, at + i)),
        spec((2, 1, 32, 16, WIDE), lambda i: (0, 0, 0, 0, at + i)),
        spec((2, 32, RADIUS, WIDE), lambda i: (0, 0, 0, i)),
        spec((2, 32, RADIUS, WIDE), lambda i: (0, 0, 0, i)),
        spec((2, RADIUS, 16, WIDE), lambda i: (0, 0, 0, at + i)),
        spec((2, RADIUS, 16, WIDE), lambda i: (0, 0, 0, at + i)),
        spec((2, 2, RADIUS, RADIUS, WIDE), lambda i: (0, 0, 0, 0, i)),
        spec((2, RADIUS, RADIUS, WIDE), lambda i: (0, 0, 0, at + i)),
        spec((2, RADIUS, RADIUS, WIDE), lambda i: (0, 0, 0, at + i)),
    ]
    args = [flip, queries, own, *sides, *rows, corner, *far_sides]
    in_specs += [spec((8, 8, WIDE), lambda i: (0, 0, at + i))] * (2 * PIECES)
    in_specs += [
        spec((512, HD), lambda i: (0, 0)),
        spec((48, 32, HD), lambda i: (0, 0, 0)),
    ]
    args += [*text, *feats]
    aliases = {}
    if output is not None:
        aliases = {len(args): 0}
        in_specs.append(spec(memory_space=pl.ANY))
        args.append(output)
    in_specs += [spec(memory_space=pl.ANY)] * len(deps)
    args += deps
    return pl.pallas_call(
        functools.partial(attend_body, len(deps) + (output is not None)),
        grid=(heads // PER_STEP,),
        in_specs=in_specs,
        out_specs=spec((1, 32, 16, WIDE), lambda i: (0, 0, 0, at + i)),
        out_shape=jax.ShapeDtypeStruct(queries.shape, jnp.bfloat16),
        scratch_shapes=[
            pltpu.VMEM((48, 32, 2 * HD), jnp.bfloat16),
            pltpu.VMEM((48, 32, 2 * HD), jnp.bfloat16),
            pltpu.VMEM((512, 2 * HD), jnp.bfloat16),
        ],
        input_output_aliases=aliases,
        compiler_params=pltpu.CompilerParams(vmem_limit_bytes=VMEM_LIMIT),
        cost_estimate=pl.CostEstimate(
            flops=1000, bytes_accessed=1000, transcendentals=0
        ),
    )(*args)


def features():
    query = np.arange(512)
    lane = np.arange(HD)
    hot = (
        (lane[None] == (query % 16)[:, None])
        | (lane[None] - 16 == (query // 16)[:, None])
        | (lane[None] == 48)
    )
    row = jnp.arange(48, dtype=jnp.int32)[:, None, None] - RADIUS
    col = jnp.arange(32, dtype=jnp.int32)[None, :, None] - RADIUS
    lane = jnp.arange(HD, dtype=jnp.int32)[None, None, :]
    grid_row = lax.axis_index("lat") * 32 + row
    bad = (lane < 16) & (jnp.abs(col - lane) > RADIUS)
    bad |= (lane >= 16) & (lane < 48) & (jnp.abs(row - (lane - 16)) > RADIUS)
    bad |= (lane == 48) & ((grid_row < 0) | (grid_row >= N_LAT * 32))
    return jnp.asarray(hot, jnp.bfloat16), jnp.where(bad, NEG, 0.0).astype(jnp.bfloat16)


def on_device(queries, key_value, text_kv):
    flip = (lax.axis_index("lat") % CORE).astype(jnp.int32)[None]
    starts = [sum(CHUNKS[:i]) for i in range(len(CHUNKS))]
    feats = features()
    corners = [None] * len(CHUNKS)

    def inner(a, b):
        return a != b

    def send_corners(i, deps):
        rows = pack_corners(flip, *sides[i], deps)
        corners[i] = send(rows, core=1)
        return rows

    sides = []

    def send_sides(i, deps):
        r, l = pack_sides(key_value, starts[i], CHUNKS[i], deps)
        sides.append((send_lon(r, 1), send_lon(l, -1)))
        return r

    by_z = [send(text_kv, zl=1), send(text_kv, zh=1), send(text_kv, zh=1, zl=1)]
    block = prompt_stack(text_kv, by_z, ())
    by_y = [send(block, y=step) for step in (1, 3, 2)]
    near, far = pack_rows(flip, key_value, (block,))
    mine, theirs = prompt_split(flip, block, by_y, (near,))
    other = send(theirs, core=1)
    near, far = send(near, core=1), send_where(far, inner, zh=1, core=1)
    up, down = [send(x, x_=1) for x in (mine, other)], [send(x, x_=3) for x in (mine, other)]
    pieces = [mine, other, *up, *down, send(up[0], x_=1), send(down[1], x_=3)]
    swapped = [send(piece, core=1) for piece in pieces]
    text = pieces + [swapped[i ^ 1] for i in range(PIECES)]
    token = send_sides(0, (up[0], down[1]))
    token = send_sides(1, (token,))
    r, l = pack_far_sides(far, (token,))
    far_sides = (send_where(r, inner, lon=1), send_where(l, inner, lon=-1))
    token = send_sides(2, (r,))
    token = send_sides(3, (token,))
    output = None
    for i in range(len(CHUNKS)):
        token = send_corners(i, (token,))
        output = token = attend(
            flip, queries, key_value, sides[i], (near, far), corners[i], far_sides, text, feats,
            output, starts[i], CHUNKS[i], (),
        )
    return output


def solution(mesh):
    in_specs = (
        P(None, "lat", "lon", None),
        P(None, None, "lat", "lon", None),
        P(None, None, ("lat", "lon"), None),
    )
    out_specs = P(None, "lat", "lon", None)
    return jax.shard_map(
        on_device, mesh=mesh, in_specs=in_specs, out_specs=out_specs, check_vma=False
    )
```

```python
import functools
import math

import jax
import jax.numpy as jnp
import numpy as np
from jax import lax
from jax.experimental import pallas as pl
from jax.experimental.pallas import tpu as pltpu
from jax.sharding import PartitionSpec as P

HD = 128
RADIUS = 8
NEG = -1e30
ZH, CORE, NX, ZL, NY = 2, 2, 4, 2, 4
N_LAT, N_LON = ZH * CORE, NX * ZL * NY
CHUNKS = (8, 8, 4, 4)
PER_STEP = 4
WIDE = PER_STEP * HD
BLOCK = 16
VMEM_LIMIT = 66_800_000
PIECES = 8


def send_where(x, use, zh=0, core=0, lon=0):
    pairs = []
    for i in range(N_LAT * N_LON):
        lat, at = divmod(i, N_LON)
        a, b = divmod(lat, CORE)
        if use(a, b):
            lat = (a + zh) % ZH * CORE + (b + core) % CORE
            pairs.append((i, lat * N_LON + (at + lon) % N_LON))
    return lax.ppermute(x, ("lat", "lon"), pairs)


def send(x, zh=0, core=0, x_=0, zl=0, y=0):
    pairs = []
    for i in range(N_LAT * N_LON):
        c = list(np.unravel_index(i, (ZH, CORE, NX, ZL, NY)))
        t = [(a + b) % n for a, b, n in zip(c, (zh, core, x_, zl, y), (ZH, CORE, NX, ZL, NY))]
        pairs.append((i, int(np.ravel_multi_index(t, (ZH, CORE, NX, ZL, NY)))))
    return lax.ppermute(x, ("lat", "lon"), pairs)


def send_lon(x, step):
    return lax.ppermute(x, "lon", [(i, (i + step) % N_LON) for i in range(N_LON)])


def glue(body, out_shapes, args, deps, specs=None, out_specs=None, grid=None):
    if specs is None:
        specs = [pl.BlockSpec(memory_space=pltpu.VMEM)] * len(args)
        out_specs = [pl.BlockSpec(memory_space=pltpu.VMEM)] * len(out_shapes)
    count = len(args)

    def kernel(*refs):
        body(*refs[:count], *refs[count + len(deps) :])

    return pl.pallas_call(
        kernel,
        grid=grid or (),
        in_specs=list(specs) + [pl.BlockSpec(memory_space=pl.ANY)] * len(deps),
        out_specs=out_specs,
        out_shape=[jax.ShapeDtypeStruct(shape, jnp.bfloat16) for shape in out_shapes],
        compiler_params=pltpu.CompilerParams(vmem_limit_bytes=VMEM_LIMIT),
        cost_estimate=pl.CostEstimate(flops=1000, bytes_accessed=1000, transcendentals=0),
    )(*args, *deps)


def pack_sides(own, head, heads, deps):
    wide = 4 * HD
    at = head * HD // wide

    def body(own_ref, r_ref, l_ref):
        r_ref[...] = own_ref[:, 0, :, RADIUS:]
        l_ref[...] = own_ref[:, 0, :, :RADIUS]

    specs = [pl.BlockSpec((2, 1, 32, 16, wide), lambda i: (0, 0, 0, 0, at + i))]
    out_specs = [pl.BlockSpec((2, 32, RADIUS, wide), lambda i: (0, 0, 0, i))] * 2
    shape = (2, 32, RADIUS, heads * HD)
    return glue(body, [shape] * 2, [own], deps, specs, out_specs, (heads * HD // wide,))


def carry(arrays, deps):
    def body(*refs):
        for src, dst in zip(refs[: len(arrays)], refs[len(arrays) :]):
            dst[...] = src[...]

    return glue(body, [x.shape for x in arrays], list(arrays), deps)


def pack_far_sides(far, deps):
    def body(far_ref, r_ref, l_ref):
        r_ref[...] = far_ref[:, :, RADIUS:]
        l_ref[...] = far_ref[:, :, :RADIUS]

    specs = [pl.BlockSpec((2, RADIUS, 16, 3072), lambda i: (0, 0, 0, i))]
    out_specs = [pl.BlockSpec((2, RADIUS, RADIUS, 3072), lambda i: (0, 0, 0, i))] * 2
    return glue(body, [(2, RADIUS, RADIUS, 3072)] * 2, [far], deps, specs, out_specs, (1,))


def pack_rows(flip, own, deps):
    def body(flip_ref, first_ref, last_ref, near_ref, far_ref):
        odd = flip_ref[0] == 1
        near_ref[...] = jnp.where(odd, first_ref[:, 0], last_ref[:, 0])
        far_ref[...] = jnp.where(odd, last_ref[:, 0], first_ref[:, 0])

    specs = [
        pl.BlockSpec(memory_space=pltpu.SMEM),
        pl.BlockSpec((2, 1, RADIUS, 16, 1024), lambda i: (0, 0, 0, 0, i)),
        pl.BlockSpec((2, 1, RADIUS, 16, 1024), lambda i: (0, 0, 3, 0, i)),
    ]
    out_specs = [pl.BlockSpec((2, RADIUS, 16, 1024), lambda i: (0, 0, 0, i))] * 2
    return glue(body, [(2, RADIUS, 16, 3072)] * 2, [flip, own, own], deps, specs, out_specs, (3,))


def pack_corners(flip, left, right, deps):
    width = left.shape[-1]

    def body(flip_ref, lt_ref, lb_ref, rt_ref, rb_ref, out_ref):
        odd = flip_ref[0] == 1
        out_ref[0] = jnp.where(odd, lt_ref[...], lb_ref[...])
        out_ref[1] = jnp.where(odd, rt_ref[...], rb_ref[...])

    at_first = pl.BlockSpec((2, RADIUS, RADIUS, width), lambda i: (0, 0, 0, i))
    at_last = pl.BlockSpec((2, RADIUS, RADIUS, width), lambda i: (0, 3, 0, i))
    return glue(
        body,
        [(2, 2, RADIUS, RADIUS, width)],
        [flip, left, left, right, right],
        deps,
        [pl.BlockSpec(memory_space=pltpu.SMEM), at_first, at_last, at_first, at_last],
        [pl.BlockSpec((2, 2, RADIUS, RADIUS, width), lambda i: (0, 0, 0, 0, i))],
        (1,),
    )[0]


def prompt_stack(text, others, deps):
    def body(*refs):
        for i, ref in enumerate(refs[:-1]):
            refs[-1][i] = ref[:, 0]

    return glue(body, [(4, 2, 4, 3072)], [text, *others], deps)[0]


def prompt_split(flip, block, others, deps):
    def body(flip_ref, *refs):
        mine_ref, theirs_ref = refs[-2:]
        odd = flip_ref[0] == 1
        for half in (0, 1):
            a_ref, b_ref = refs[2 * half : 2 * half + 2]
            for i in range(4):
                keys = jnp.concatenate([a_ref[i, 0], b_ref[i, 0]], axis=0)
                values = jnp.concatenate([a_ref[i, 1], b_ref[i, 1]], axis=0)
                mine_ref[4 * half + i] = jnp.where(odd, values, keys)
                theirs_ref[4 * half + i] = jnp.where(odd, keys, values)

    whole = pl.BlockSpec(memory_space=pltpu.VMEM)
    return glue(
        body,
        [(8, 8, 3072)] * 2,
        [flip, block, *others],
        deps,
        [pl.BlockSpec(memory_space=pltpu.SMEM)] + [whole] * 4,
        [whole] * 2,
    )


def attend_body(unused, *refs):
    refs = list(refs)
    flip_ref, q_ref, own_ref, left_ref, right_ref, near_ref, far_ref = refs[:7]
    corner_ref, far_left_ref, far_right_ref = refs[7:10]
    del refs[:10]
    ta_refs, tb_refs = refs[:PIECES], refs[PIECES : 2 * PIECES]
    del refs[: 2 * PIECES]
    e_ref, f_ref = refs[:2]
    del refs[:2]
    del refs[:unused]
    o_ref, keys_s, vals_s, tvals_s = refs
    rows, cols = 32, 16

    @pl.when(pl.program_id(0) == 0)
    def _():
        keys_s[:, :, HD:] = f_ref[...]
        vals_s[:, :, HD:] = jnp.ones((48, 32, HD), jnp.bfloat16)
        tvals_s[:, HD:] = jnp.ones((512, HD), jnp.bfloat16)

    scale = math.log2(math.e) / math.sqrt(HD)
    nt = (((1,), (1,)), ((), ()))
    flip = flip_ref[0] == 1
    for head in range(PER_STEP):
        hs = slice(head * HD, (head + 1) * HD)
        for kv, dst in ((0, keys_s), (1, vals_s)):
            left, right = left_ref[kv, :, :, hs], right_ref[kv, :, :, hs]
            own = own_ref[kv, 0, :, :, hs]
            dst[8:40, :, :HD] = jnp.concatenate([left, own, right], axis=1)
            near = [corner_ref[0, kv, :, :, hs], near_ref[kv, :, :, hs], corner_ref[1, kv, :, :, hs]]
            far = [far_left_ref[kv, :, :, hs], far_ref[kv, :, :, hs], far_right_ref[kv, :, :, hs]]
            near, far = jnp.concatenate(near, axis=1), jnp.concatenate(far, axis=1)
            dst[0:8, :, :HD] = jnp.where(flip, near, far)
            dst[40:48, :, :HD] = jnp.where(flip, far, near)
        a = jnp.concatenate([ref[:, :, hs].reshape(64, HD) for ref in ta_refs], axis=0)
        b = jnp.concatenate([ref[:, :, hs].reshape(64, HD) for ref in tb_refs], axis=0)
        text_keys = jnp.where(flip, b, a)
        tvals_s[:, :HD] = jnp.where(flip, a, b)
        for r in range(rows // BLOCK):
            q = q_ref[0, r * BLOCK : (r + 1) * BLOCK, :, hs].reshape(BLOCK * cols, HD)
            q_wide = jnp.concatenate([q, e_ref[r * BLOCK * cols : (r + 1) * BLOCK * cols]], axis=1)
            span = BLOCK + 2 * RADIUS
            keys = keys_s[r * BLOCK : r * BLOCK + span].reshape(span * 32, 2 * HD)
            vals = vals_s[r * BLOCK : r * BLOCK + span].reshape(span * 32, 2 * HD)
            near = lax.dot_general(q_wide, keys, nt, preferred_element_type=jnp.float32)
            far = lax.dot_general(q, text_keys, nt, preferred_element_type=jnp.float32)
            top = jnp.maximum(
                jnp.max(near, -1, keepdims=True), jnp.max(far, -1, keepdims=True)
            )
            near = jnp.exp2((near - top) * scale).astype(jnp.bfloat16)
            far = jnp.exp2((far - top) * scale).astype(jnp.bfloat16)
            out = jnp.dot(near, vals, preferred_element_type=jnp.float32)
            out = out + jnp.dot(far, tvals_s[...], preferred_element_type=jnp.float32)
            out = (out[:, :HD] / out[:, HD:]).astype(jnp.bfloat16)
            o_ref[0, r * BLOCK : (r + 1) * BLOCK, :, hs] = out.reshape(BLOCK, cols, HD)


def attend(flip, queries, own, sides, rows, corner, far_sides, text, feats, output, head, heads, deps):
    at = head // PER_STEP
    spec = pl.BlockSpec
    in_specs = [
        spec(memory_space=pltpu.SMEM),
        spec((1, 32, 16, WIDE), lambda i: (0, 0, 0, at + i)),
        spec((2, 1, 32, 16, WIDE), lambda i: (0, 0, 0, 0, at + i)),
        spec((2, 32, RADIUS, WIDE), lambda i: (0, 0, 0, i)),
        spec((2, 32, RADIUS, WIDE), lambda i: (0, 0, 0, i)),
        spec((2, RADIUS, 16, WIDE), lambda i: (0, 0, 0, at + i)),
        spec((2, RADIUS, 16, WIDE), lambda i: (0, 0, 0, at + i)),
        spec((2, 2, RADIUS, RADIUS, WIDE), lambda i: (0, 0, 0, 0, i)),
        spec((2, RADIUS, RADIUS, WIDE), lambda i: (0, 0, 0, at + i)),
        spec((2, RADIUS, RADIUS, WIDE), lambda i: (0, 0, 0, at + i)),
    ]
    args = [flip, queries, own, *sides, *rows, corner, *far_sides]
    in_specs += [spec((8, 8, WIDE), lambda i: (0, 0, at + i))] * (2 * PIECES)
    in_specs += [
        spec((512, HD), lambda i: (0, 0)),
        spec((48, 32, HD), lambda i: (0, 0, 0)),
    ]
    args += [*text, *feats]
    aliases = {}
    if output is not None:
        aliases = {len(args): 0}
        in_specs.append(spec(memory_space=pl.ANY))
        args.append(output)
    in_specs += [spec(memory_space=pl.ANY)] * len(deps)
    args += deps
    return pl.pallas_call(
        functools.partial(attend_body, len(deps) + (output is not None)),
        grid=(heads // PER_STEP,),
        in_specs=in_specs,
        out_specs=spec((1, 32, 16, WIDE), lambda i: (0, 0, 0, at + i)),
        out_shape=jax.ShapeDtypeStruct(queries.shape, jnp.bfloat16),
        scratch_shapes=[
            pltpu.VMEM((48, 32, 2 * HD), jnp.bfloat16),
            pltpu.VMEM((48, 32, 2 * HD), jnp.bfloat16),
            pltpu.VMEM((512, 2 * HD), jnp.bfloat16),
        ],
        input_output_aliases=aliases,
        compiler_params=pltpu.CompilerParams(vmem_limit_bytes=VMEM_LIMIT),
        cost_estimate=pl.CostEstimate(
            flops=1000, bytes_accessed=1000, transcendentals=0
        ),
    )(*args)


def features():
    query = np.arange(512)
    lane = np.arange(HD)
    hot = (
        (lane[None] == (query % 16)[:, None])
        | (lane[None] - 16 == (query // 16)[:, None])
        | (lane[None] == 48)
    )
    row = jnp.arange(48, dtype=jnp.int32)[:, None, None] - RADIUS
    col = jnp.arange(32, dtype=jnp.int32)[None, :, None] - RADIUS
    lane = jnp.arange(HD, dtype=jnp.int32)[None, None, :]
    grid_row = lax.axis_index("lat") * 32 + row
    bad = (lane < 16) & (jnp.abs(col - lane) > RADIUS)
    bad |= (lane >= 16) & (lane < 48) & (jnp.abs(row - (lane - 16)) > RADIUS)
    bad |= (lane == 48) & ((grid_row < 0) | (grid_row >= N_LAT * 32))
    return jnp.asarray(hot, jnp.bfloat16), jnp.where(bad, NEG, 0.0).astype(jnp.bfloat16)


def on_device(queries, key_value, text_kv):
    flip = (lax.axis_index("lat") % CORE).astype(jnp.int32)[None]
    starts = [sum(CHUNKS[:i]) for i in range(len(CHUNKS))]
    feats = features()
    corners = [None] * len(CHUNKS)

    def inner(a, b):
        return a != b

    def send_corners(i, deps):
        rows = pack_corners(flip, *sides[i], deps)
        corners[i] = send(rows, core=1)
        return rows

    sides = []

    def send_sides(i, deps):
        r, l = pack_sides(key_value, starts[i], CHUNKS[i], deps)
        sides.append((send_lon(r, 1), send_lon(l, -1)))
        return r

    by_z = [send(text_kv, zl=1), send(text_kv, zh=1), send(text_kv, zh=1, zl=1)]
    block = prompt_stack(text_kv, by_z, ())
    by_y = [send(block, y=step) for step in (1, 3, 2)]
    near, far = pack_rows(flip, key_value, (block,))
    mine, theirs = prompt_split(flip, block, by_y, (near,))
    other = send(theirs, core=1)
    near, far = send(near, core=1), send_where(far, inner, zh=1, core=1)
    up, down = [send(x, x_=1) for x in (mine, other)], [send(x, x_=3) for x in (mine, other)]
    pieces = [mine, other, *up, *down, send(up[0], x_=1), send(down[1], x_=3)]
    swapped = [send(piece, core=1) for piece in pieces]
    text = pieces + [swapped[i ^ 1] for i in range(PIECES)]
    token = send_sides(0, (up[0], down[1]))
    token = send_sides(1, (token,))
    r, l = pack_far_sides(far, (token,))
    far_sides = (send_where(r, inner, lon=1), send_where(l, inner, lon=-1))
    token = send_sides(2, (r,))
    token = send_sides(3, (token,))
    output = None
    for i in range(len(CHUNKS)):
        token = send_corners(i, (token,))
        output = token = attend(
            flip, queries, key_value, sides[i], (near, far), corners[i], far_sides, text, feats,
            output, starts[i], CHUNKS[i], (),
        )
    return output


def solution(mesh):
    in_specs = (
        P(None, "lat", "lon", None),
        P(None, None, "lat", "lon", None),
        P(None, None, ("lat", "lon"), None),
    )
    out_specs = P(None, "lat", "lon", None)
    return jax.shard_map(
        on_device, mesh=mesh, in_specs=in_specs, out_specs=out_specs, check_vma=False
    )
```
